32 devices in a mesh: ens: 4 (over z), tile: 8 (over y, x, core).
Axes of the slice: x: 2, y: 2, z: 4, core: 2. Of those that a mesh axis runs over, the one named last changes fastest.
Arguments:
- conditioning: bfloat16 [12, 64, 128], P(None, 'tile'), may hold values from -6 to 6
- member_noise: float32 [4, 4, 64, 128], P('ens', None, 'tile'), may hold values from -6 to 6
- reg_in: bfloat16 [3, 3, 12, 128], replicated, may hold values from -1 to 1
- reg_down: bfloat16 [3, 3, 128, 128], replicated, may hold values from -0.25 to 0.25
- reg_low: bfloat16 [3, 3, 128, 128], replicated, may hold values from -0.25 to 0.25
- reg_up: bfloat16 [4, 4, 128, 128], replicated, may hold values from -0.375 to 0.375
- reg_fine: bfloat16 [3, 3, 128, 128], replicated, may hold values from -0.25 to 0.25
- reg_out: bfloat16 [3, 3, 4, 128], replicated, may hold values from -0.3125 to 0.3125
- dif_in: bfloat16 [3, 3, 20, 128], replicated, may hold values from -0.75 to 0.75
- dif_down: bfloat16 [3, 3, 128, 128], replicated, may hold values from -0.25 to 0.25
- dif_low: bfloat16 [3, 3, 128, 128], replicated, may hold values from -0.25 to 0.25
- dif_up: bfloat16 [4, 4, 128, 128], replicated, may hold values from -0.375 to 0.375
- dif_fine: bfloat16 [3, 3, 128, 128], replicated, may hold values from -0.25 to 0.25
- dif_out: bfloat16 [3, 3, 4, 128], replicated, may hold values from -0.3125 to 0.3125
Outputs:
- prediction: float32 [4, 4, 64, 128], P('ens', None, 'tile')
The draws below stay inside these ranges and needn't reach their ends.
All inputs are finite; a program needn't handle non-finite values.
Results may differ from the reference program's by a relative error of at most 0.015.
Values may be sent and summed in bfloat16 or wider, within the bound.
A program may use at most 64 MiB of HBM per device.

```python
import jax
import jax.numpy as jnp
from jax import lax

C = 128
OUTC = 4
CIREG = 12
STEPS = 2
W = 128
CIN = 20
H = 64
ENS = 4


def levels(rng, extent, cuts, low, top_value):
    def one(position, parts):
        heights = jax.random.uniform(jax.random.fold_in(jax.random.fold_in(rng, 6), position), (parts,), jnp.float32, low / len(cuts), top_value / len(cuts))
        return jnp.repeat(jnp.exp(heights), extent[position] // parts).reshape((-1,) + (1,) * (len(extent) - position - 1))

    loudness = one(*cuts[0])
    for cut in cuts[1:]:
        loudness = loudness * one(*cut)
    return loudness


def normal_values(key, shape, scale, bound, cuts=(), kind=jnp.bfloat16):
    result = jax.random.normal(key, shape, jnp.float32) * scale
    if len(cuts) > 0:
        result = levels(key, shape, cuts, -0.22, 0.18) * result
    return jnp.clip(result, min=-bound, max=bound).astype(kind)


def setup_inputs(seed: int = 0) -> dict:
    key_list = jax.random.split(jax.random.key(seed), 15)
    return {
        "conditioning": normal_values(key_list[0], (CIREG, H, W), 1.0, 6.0, ((1, 8),)),
        "member_noise": normal_values(key_list[1], (ENS, OUTC, H, W), 1.0, 6.0, ((0, 4), (2, 8)), jnp.float32),
        "reg_in": normal_values(key_list[2], (3, 3, CIREG, C), (3 * CIREG) ** -0.5, 1.0),
        "reg_down": normal_values(key_list[3], (3, 3, C, C), (4 * C) ** -0.5, 0.25),
        "reg_low": normal_values(key_list[4], (3, 3, C, C), (4 * C) ** -0.5, 0.25),
        "reg_up": normal_values(key_list[5], (4, 4, C, C), (2 * C) ** -0.5, 0.375),
        "reg_fine": normal_values(key_list[6], (3, 3, C, C), (4 * C) ** -0.5, 0.25),
        "reg_out": normal_values(key_list[7], (3, 3, OUTC, C), (3 * C) ** -0.5, 0.3125),
        "dif_in": normal_values(key_list[8], (3, 3, CIN, C), (3 * CIN) ** -0.5, 0.75),
        "dif_down": normal_values(key_list[9], (3, 3, C, C), (4 * C) ** -0.5, 0.25),
        "dif_low": normal_values(key_list[10], (3, 3, C, C), (4 * C) ** -0.5, 0.25),
        "dif_up": normal_values(key_list[11], (4, 4, C, C), (2 * C) ** -0.5, 0.375),
        "dif_fine": normal_values(key_list[12], (3, 3, C, C), (4 * C) ** -0.5, 0.25),
        "dif_out": normal_values(key_list[13], (3, 3, OUTC, C), (3 * C) ** -0.5, 0.3125),
    }


sigma_top = 1.0
sigma_ratio = 0.4
sigma_data = 0.5

def silu_round(values):
    return jax.nn.silu(values).astype(jnp.bfloat16)

def conv_fields(padded, weight):
    height = padded.shape[1] - 2
    across = padded.shape[2] - 2
    running = None
    for tap_y in range(3):
        for tap_x in range(3):
            window = padded[:, tap_y:tap_y + height, tap_x:tap_x + across].astype(jnp.float32)
            tap_term = jnp.einsum('crw,co->rwo', window, weight[tap_y, tap_x].astype(jnp.float32))
            running = tap_term if running is None else running + tap_term
    return running

def conv_feat(padded, weight, stride):
    count_y = (padded.shape[0] - 3) // stride + 1
    count_x = (padded.shape[1] - 3) // stride + 1
    running = None
    for tap_y in range(3):
        for tap_x in range(3):
            window = padded[tap_y:tap_y + stride * (count_y - 1) + 1:stride, tap_x:tap_x + stride * (count_x - 1) + 1:stride]
            tap_term = jnp.einsum('rwc,co->rwo', window.astype(jnp.float32), weight[tap_y, tap_x].astype(jnp.float32))
            running = tap_term if running is None else running + tap_term
    return running

def conv_out(padded, weight):
    height = padded.shape[0] - 2
    across = padded.shape[1] - 2
    running = None
    for tap_y in range(3):
        for tap_x in range(3):
            window = padded[tap_y:tap_y + height, tap_x:tap_x + across].astype(jnp.float32)
            tap_term = jnp.einsum('rwc,oc->orw', window, weight[tap_y, tap_x].astype(jnp.float32))
            running = tap_term if running is None else running + tap_term
    return running

def up_conv(padded, weight):
    count_y = padded.shape[0] - 2
    count_x = padded.shape[1] - 2
    tap_pairs = (((1, 1), (0, 3)), ((2, 0), (1, 2)))

    def parity(side_y, side_x):
        running = None
        for offset_y, kernel_y in tap_pairs[side_y]:
            for offset_x, kernel_x in tap_pairs[side_x]:
                window = padded[offset_y:offset_y + count_y, offset_x:offset_x + count_x].astype(jnp.float32)
                tap_term = jnp.einsum('rwc,co->rwo', window, weight[kernel_y, kernel_x].astype(jnp.float32))
                running = tap_term if running is None else running + tap_term
        return running
    upper_rows = jnp.stack([parity(0, 0), parity(0, 1)], axis=2)
    lower_rows = jnp.stack([parity(1, 0), parity(1, 1)], axis=2)
    merged = jnp.stack([upper_rows, lower_rows], axis=1)
    return merged.reshape(2 * count_y, 2 * count_x, merged.shape[-1])

def feat_pad(values):
    return jnp.pad(values, ((1, 1), (1, 1), (0, 0)))

def network_pass(padded_fields, weights):
    in_weight, down_weight, low_weight, up_weight, fine_weight, out_weight = weights
    top_level = silu_round(conv_fields(padded_fields, in_weight))
    coarse = silu_round(conv_feat(feat_pad(top_level), down_weight, 2))
    middle = silu_round(conv_feat(feat_pad(coarse), low_weight, 1))
    upward = up_conv(feat_pad(middle), up_weight)
    summed = (top_level.astype(jnp.float32) + upward).astype(jnp.bfloat16)
    refined = silu_round(conv_feat(feat_pad(summed), fine_weight, 1))
    return conv_out(feat_pad(refined), out_weight)

def reference(conditioning, member_noise, reg_in, reg_down, reg_low, reg_up, reg_fine, reg_out, dif_in, dif_down, dif_low, dif_up, dif_fine, dif_out):
    field_pad = ((0, 0), (1, 1), (1, 1))
    reg_mean = network_pass(jnp.pad(conditioning, field_pad), (reg_in, reg_down, reg_low, reg_up, reg_fine, reg_out))
    dif_weights = (dif_in, dif_down, dif_low, dif_up, dif_fine, dif_out)

    def member_run(noise_one):
        residual_field = sigma_top * noise_one.astype(jnp.float32)
        for step_index in range(STEPS):
            sigma_now = sigma_top * sigma_ratio ** step_index
            sigma_next = sigma_top * sigma_ratio ** (step_index + 1) if step_index + 1 < STEPS else 0.0
            scale_sq = sigma_now ** 2 + sigma_data ** 2
            in_gain = 1.0 / math_sqrt(scale_sq)
            skip_gain = sigma_data ** 2 / scale_sq
            out_gain = sigma_now * sigma_data / math_sqrt(scale_sq)
            inputs = jnp.concatenate([(in_gain * residual_field).astype(jnp.bfloat16), conditioning, reg_mean.astype(jnp.bfloat16)], axis=0)
            network = network_pass(jnp.pad(inputs, field_pad), dif_weights)
            denoised = skip_gain * residual_field + out_gain * network
            residual_field = residual_field + (sigma_next - sigma_now) / sigma_now * (residual_field - denoised)
        return reg_mean + residual_field
    return lax.map(member_run, member_noise)

def math_sqrt(number):
    return number ** 0.5
```

```python
import functools

import jax
import jax.numpy as jnp
from jax import lax
from jax.experimental import pallas as pl
from jax.experimental.pallas import tpu as pltpu
from jax.sharding import PartitionSpec as P

STEPS = 2
sigma_top = 1.0
sigma_ratio = 0.4
sigma_data = 0.5

F32 = jnp.float32
BF16 = jnp.bfloat16
HIGH = lax.Precision.HIGHEST
TILE = 8
REACH = 2


def step_gains(k):
    now = sigma_top * sigma_ratio**k
    later = sigma_top * sigma_ratio ** (k + 1) if k + 1 < STEPS else 0.0
    sq = now**2 + sigma_data**2
    return 1.0 / sq**0.5, sigma_data**2 / sq, now * sigma_data / sq**0.5, (later - now) / now


def iota2(shape, dim):
    return lax.broadcasted_iota(jnp.int32, shape, dim)


def one_hot(cond, kind=BF16):
    return jnp.where(cond, 1.0, 0.0).astype(kind)


def silu(v):
    h = 0.5 * v
    return h + h * jnp.tanh(h)


def lane_left(z):
    cols = z.shape[-1]
    half = cols // 2
    lane = iota2(z.shape, 1)
    low = jnp.where(lane == 0, 0.0, pltpu.roll(z, half + 1, 1))
    return jnp.where(lane < half, low, pltpu.roll(z, half, 1))


def lane_right(z):
    cols = z.shape[-1]
    half = cols // 2
    lane = iota2(z.shape, 1)
    high = jnp.where(lane == cols - 1, 0.0, pltpu.roll(z, half - 1, 1))
    return jnp.where(lane < half, pltpu.roll(z, half, 1), high)


def down_one(x):
    return jnp.where(iota2(x.shape, 0) == 0, 0.0, pltpu.roll(x, 1, 0))


def up_one(x):
    n = x.shape[0]
    return jnp.where(iota2(x.shape, 0) == n - 1, 0.0, pltpu.roll(x, n - 1, 0))


def store_fine(ref, row, even, odd):
    half, ch = even.shape
    e, o = even.astype(BF16), odd.astype(BF16)
    ref[row, :half, 0:ch] = down_one(odd).astype(BF16)
    ref[row, half:, 0:ch] = e
    ref[row, :half, ch : 2 * ch] = e
    ref[row, half:, ch : 2 * ch] = o
    ref[row, :half, 2 * ch :] = o
    ref[row, half:, 2 * ch :] = up_one(even).astype(BF16)


def store_coarse(ref, row, v):
    ch = v.shape[1]
    ref[row, :, 0:ch] = down_one(v).astype(BF16)
    ref[row, :, ch : 2 * ch] = v.astype(BF16)
    ref[row, :, 2 * ch :] = up_one(v).astype(BF16)


def dot(a, b):
    return jnp.dot(a, b, preferred_element_type=F32)


def kernel(n, cols, *refs):
    (cond_ref, noise_ref, rin_ref, rdown_h, rlow_h, rup_h, rfine_h, rout_ref,
     din_ref, ddown_h, dlow_h, dup_h, dfine_h, dout_ref, out_ref,
     rdown, rlow, rup, rfine, ddown, dlow, dup, dfine,
     rin, rall, din, dall,
     condb, noiseb, resb, fields, top, coarse, middle, joined, zbuf, mean, res,
     wsem, csend, crecv, nsend, nrecv, rsend, rrecv) = refs
    me = lax.axis_index("tile")
    half = cols // 2
    ch = 128
    loads = [
        pltpu.make_async_copy(src, dst, wsem.at[i])
        for i, (src, dst) in enumerate(
            [(rdown_h, rdown), (rlow_h, rlow), (rup_h, rup), (rfine_h, rfine),
             (ddown_h, ddown), (dlow_h, dlow), (dup_h, dup), (dfine_h, dfine)]
        )
    ]
    offsets = [d for d in range(-REACH, REACH + 1) if d != 0]

    def there(d):
        return (me + d >= 0) & (me + d < n)

    barrier = pltpu.get_barrier_semaphore()
    for d in offsets:
        @pl.when(there(d))
        def _():
            pl.semaphore_signal(barrier, inc=1, device_id={"tile": me + d},
                                device_id_type=pl.DeviceIdType.MESH)
    for copy in loads:
        copy.start()

    perm = one_hot(iota2((cols, cols), 0) == 2 * (iota2((cols, cols), 1) % half) + iota2((cols, cols), 1) // half)
    perm_f = perm.astype(F32)
    nch = cond_ref.shape[0]
    shape = (TILE * 16, nch * TILE)
    m, k = iota2(shape, 0), iota2(shape, 1)
    gather = one_hot(k == (m % 16) * TILE + m // 16)
    gather = jnp.where(m % 16 < nch, gather.astype(F32), 0.0).astype(BF16)
    own = cond_ref[...].astype(F32).reshape(nch * TILE, cols).astype(BF16)
    own = dot(gather, dot(own, perm).astype(BF16)).astype(BF16)
    condb[REACH] = own.reshape(TILE, 16, cols)
    shape = (TILE * 8, 4 * TILE)
    m, k = iota2(shape, 0), iota2(shape, 1)
    pick = jnp.where((m % 8 < 4) & (k == (m % 8) * TILE + m // 8), 1.0, 0.0)
    noise = noise_ref[...].reshape(4 * TILE, cols)
    noise = jnp.dot(noise, perm_f, precision=HIGH, preferred_element_type=F32)
    noise = sigma_top * jnp.dot(pick, noise, precision=HIGH, preferred_element_type=F32)
    res[...] = noise
    noiseb[1] = (step_gains(0)[0] * noise).astype(BF16)
    for d in offsets:
        @pl.when(jnp.logical_not(there(d)))
        def _():
            condb[REACH + d] = jnp.zeros_like(condb[REACH + d])
            if abs(d) == 1:
                noiseb[1 + d] = jnp.zeros_like(noiseb[1 + d])
                resb[1 + d] = jnp.zeros_like(resb[1 + d])

    pl.semaphore_wait(barrier, jnp.minimum(me, REACH) + jnp.minimum(n - 1 - me, REACH))

    def cond_copy(d, incoming=False):
        return pltpu.make_async_remote_copy(
            src_ref=condb.at[REACH], dst_ref=condb.at[REACH + (d if incoming else -d)],
            send_sem=csend.at[REACH + d], recv_sem=crecv.at[REACH + (d if incoming else -d)],
            device_id={"tile": me + d}, device_id_type=pl.DeviceIdType.MESH)

    def side_copy(buf, send, recv, d, incoming=False):
        return pltpu.make_async_remote_copy(
            src_ref=buf.at[1], dst_ref=buf.at[1 + (d if incoming else -d)],
            send_sem=send.at[1 + d], recv_sem=recv.at[1 + (d if incoming else -d)],
            device_id={"tile": me + d}, device_id_type=pl.DeviceIdType.MESH)

    for d in offsets:
        @pl.when(there(d))
        def _():
            cond_copy(d).start()
    for d in (-1, 1):
        @pl.when(there(d))
        def _():
            side_copy(noiseb, nsend, nrecv, d).start()

    def place_in(src, dst, cin):
        sh = (24, cin)
        a, b = iota2(sh, 0), iota2(sh, 1)
        if cin == nch:
            take = one_hot(a == b + 8)
        else:
            want = jnp.where(b < 4, b, jnp.where(b < 4 + nch, b + 4, b - nch))
            take = one_hot(a == want)
        for y in range(3):
            parts = [dot(take, src[y, x]) for x in range(3)]
            parts.append(jnp.zeros((8, ch), F32))
            dst[y * 80 : (y + 1) * 80] = jnp.concatenate(parts, axis=0).astype(BF16)

    def place_out(src, dst, at):
        take = one_hot(iota2((8, 4), 0) == iota2((8, 4), 1) + at)
        parts = [dot(take, src[y, x]) for y in range(3) for x in range(3)]
        parts.append(jnp.zeros((8, ch), F32))
        dst[...] = jnp.concatenate(parts, axis=0).astype(BF16)

    place_in(rin_ref, rin, nch)
    place_out(rout_ref, rall, 4)
    place_in(din_ref, din, nch + 8)
    place_out(dout_ref, dall, 0)

    def put_fields(d, eight):
        wide = jnp.concatenate([eight, condb[REACH + d].astype(F32)], axis=1)
        flat = wide.reshape(TILE * 24, cols)
        left = lane_left(flat).reshape(TILE, 24, cols)
        right = lane_right(flat).reshape(TILE, 24, cols)
        both = jnp.concatenate(
            [left, wide, right, jnp.zeros((TILE, 8, cols), F32)], axis=1).astype(BF16)
        at = (REACH + d) * TILE
        fields[at : at + TILE] = both

    def unet(lo, hi, w_in, w_down, w_low, w_up, w_fine, w_all, waits):
        span = hi - lo
        first = me * TILE
        last = n * TILE

        def keep(v, g):
            return jnp.where((g + first >= 0) & (g + first < last), v, 0.0)

        def loop(count, chunk, body):
            def step(i, c):
                body(i * chunk)
                return c
            assert count % chunk == 0
            lax.fori_loop(0, count // chunk, step, 0)

        def do_top(r0):
            c = 2
            parts = []
            for i in range(c):
                parts.append(jnp.concatenate(
                    [fields[r0 + (i + y + lo + 8)] for y in range(3)], axis=0))
            lhs = jnp.concatenate(parts, axis=1)
            v = silu(lax.dot_general(lhs, w_in[...], (((0,), (0,)), ((), ())),
                                     preferred_element_type=F32))
            for i in range(c):
                u = keep(v[i * cols : (i + 1) * cols], r0 + (i + lo - 7))
                store_fine(top, r0 + i, u[:half], u[half:])

        loop(span + 14, 2, do_top)
        waits[0]()

        def do_coarse(r0):
            c = 2
            lhs = jnp.concatenate(
                [jnp.concatenate([top[2 * r0 + 2 * i + y, :half, :] for y in range(3)], axis=1)
                 for i in range(c)], axis=0)
            v = silu(dot(lhs, w_down[...]))
            for i in range(c):
                u = keep(v[i * half : (i + 1) * half], 2 * r0 + (2 * i + lo - 6))
                store_coarse(coarse, r0 + i, u)

        loop(span // 2 + 6, 2, do_coarse)
        waits[1]()

        def do_middle(r0):
            c = 4
            lhs = jnp.concatenate(
                [coarse[pl.ds(r0 + y, c)].reshape(c * half, 3 * ch) for y in range(3)], axis=1)
            v = silu(dot(lhs, w_low[...]))
            for i in range(c):
                u = keep(v[i * half : (i + 1) * half], 2 * r0 + (2 * i + lo - 4))
                store_coarse(middle, r0 + i, u)

        loop(span // 2 + 4, 4, do_middle)
        waits[2]()

        def do_joined(p0):
            c = 2
            rows = [middle[pl.ds(p0 + y, c)].reshape(c * half, 3 * ch) for y in range(3)]
            for ry, ((a, ka), (b, kb)) in enumerate((((0, 3), (1, 1)), ((1, 2), (2, 0)))):
                sums = []
                for at, kx in ((0, (3, 1)), (ch, (2, 0))):
                    lhs = jnp.concatenate(
                        [rows[a][:, at : at + 2 * ch], rows[b][:, at : at + 2 * ch]], axis=1)
                    rhs = jnp.concatenate(
                        [w_up[4 * ky + x] for ky in (ka, kb) for x in kx], axis=0)
                    sums.append(dot(lhs, rhs))
                for i in range(c):
                    t = 2 * p0 + (2 * i + ry)
                    g = t + (lo - 2)
                    base = top[t + 5, :, ch : 2 * ch].astype(F32)
                    even = keep(base[:half] + sums[0][i * half : (i + 1) * half], g)
                    odd = keep(base[half:] + sums[1][i * half : (i + 1) * half], g)
                    store_fine(joined, t, even, odd)

        loop(span // 2 + 2, 2, do_joined)
        waits[3]()

        def do_refined(r0):
            c = 2
            lhs = jnp.concatenate(
                [joined[pl.ds(r0 + y, c)].reshape(c * cols, 3 * ch) for y in range(3)], axis=1)
            v = silu(dot(lhs, w_fine[...]))
            for i in range(c):
                u = keep(v[i * cols : (i + 1) * cols], r0 + (i + lo - 1)).astype(BF16)
                zbuf[r0 + i] = lax.dot_general(
                    w_all[...], u, (((1,), (1,)), ((), ())), preferred_element_type=F32)

        loop(span + 2, 2, do_refined)
        sums = []
        for x in range(3):
            acc = None
            for y in range(3):
                s = 8 * (3 * y + x)
                term = zbuf[y : y + span, s : s + 8, :]
                acc = term if acc is None else acc + term
            sums.append(acc.reshape(span * 8, cols))
        return lane_left(sums[0]) + sums[1] + lane_right(sums[2])

    for d in offsets:
        @pl.when(there(d))
        def _():
            cond_copy(d, True).wait_recv()
    for d in range(-REACH, REACH + 1):
        put_fields(d, jnp.zeros((TILE, 8, cols), F32))
    value = unet(-TILE, 2 * TILE, rin, rdown, rlow, rup, rfine, rall,
                 [c.wait for c in loads[:4]])
    for d in (-1, 0, 1):
        part = value[(d + 1) * 64 : (d + 2) * 64]
        mean[d + 1] = jnp.where(there(d), part, 0.0)

    nothing = lambda: None
    for step in range(STEPS):
        buf, send, recv = (noiseb, nsend, nrecv) if step == 0 else (resb, rsend, rrecv)
        in_gain, skip, gain, rate = step_gains(step)
        for d in (-1, 1):
            @pl.when(there(d))
            def _():
                side_copy(buf, send, recv, d, True).wait_recv()
        for d in (-1, 0, 1):
            put_fields(d, (buf[1 + d].astype(F32) + mean[1 + d]).reshape(TILE, 8, cols))
        net = unet(0, TILE, din, ddown, dlow, dup, dfine, dall,
                   [c.wait for c in loads[4:]] if step == 0 else [nothing] * 4)
        now = res[...]
        now = now + rate * (now - (skip * now + gain * net))
        if step + 1 < STEPS:
            res[...] = now
            resb[1] = (step_gains(step + 1)[0] * now).astype(BF16)
            for d in (-1, 1):
                @pl.when(there(d))
                def _():
                    side_copy(resb, rsend, rrecv, d).start()

    total = now + mean[1]
    shape = (4 * TILE, TILE * 8)
    m, k = iota2(shape, 0), iota2(shape, 1)
    back = jnp.where((k % 4 == m // TILE) & (k // 8 == m % TILE), 1.0, 0.0)
    total = jnp.dot(back, total, precision=HIGH, preferred_element_type=F32)
    total = lax.dot_general(total, perm_f, (((1,), (1,)), ((), ())), precision=HIGH,
                            preferred_element_type=F32)
    out_ref[...] = total.reshape(1, 4, TILE, cols)

    for d in offsets:
        @pl.when(there(d))
        def _():
            cond_copy(d).wait_send()
    for d in (-1, 1):
        @pl.when(there(d))
        def _():
            side_copy(noiseb, nsend, nrecv, d).wait_send()
            side_copy(resb, rsend, rrecv, d).wait_send()


def shards(cond, noise, rin, rdown, rlow, rup, rfine, rout, din, ddown, dlow, dup, dfine, dout):
    n = lax.axis_size("tile")
    cols = cond.shape[2]
    half = cols // 2
    ch = rdown.shape[-1]
    flat = lambda w: w.reshape(-1, ch)
    taps = lambda w: w.reshape(16, ch, ch)
    vm = pl.BlockSpec(memory_space=pltpu.VMEM)
    hb = pl.BlockSpec(memory_space=pl.ANY)
    big = (9 * ch, ch)
    wide = 3 * TILE
    dma = pltpu.SemaphoreType.DMA
    return pl.pallas_call(
        functools.partial(kernel, n, cols),
        out_shape=jax.ShapeDtypeStruct(noise.shape, F32),
        in_specs=[vm, vm, vm, hb, hb, hb, hb, vm, vm, hb, hb, hb, hb, vm],
        out_specs=vm,
        scratch_shapes=[
            *[pltpu.VMEM(s, BF16) for s in (big, big, (16, ch, ch), big) * 2],
            pltpu.VMEM((240, ch), BF16),
            pltpu.VMEM((80, ch), BF16),
            pltpu.VMEM((240, ch), BF16),
            pltpu.VMEM((80, ch), BF16),
            pltpu.VMEM((2 * REACH + 1, TILE, 16, cols), BF16),
            pltpu.VMEM((3, TILE * 8, cols), BF16),
            pltpu.VMEM((3, TILE * 8, cols), BF16),
            pltpu.VMEM((5 * TILE, 80, cols), BF16),
            pltpu.VMEM((wide + 14, cols, 3 * ch), BF16),
            pltpu.VMEM((wide // 2 + 6, half, 3 * ch), BF16),
            pltpu.VMEM((wide // 2 + 4, half, 3 * ch), BF16),
            pltpu.VMEM((wide + 4, cols, 3 * ch), BF16),
            pltpu.VMEM((wide + 2, 80, cols), F32),
            pltpu.VMEM((3, TILE * 8, cols), F32),
            pltpu.VMEM((TILE * 8, cols), F32),
            dma((8,)), dma((5,)), dma((5,)), dma((3,)), dma((3,)), dma((3,)), dma((3,)),
        ],
        compiler_params=pltpu.CompilerParams(
            collective_id=0, has_side_effects=True, vmem_limit_bytes=48 * 1024 * 1024
        ),
        cost_estimate=pl.CostEstimate(flops=4 * 10**9, bytes_accessed=3 * 10**6, transcendentals=2 * 10**6),
    )(cond, noise, rin, flat(rdown), flat(rlow), taps(rup), flat(rfine), rout,
      din, flat(ddown), flat(dlow), taps(dup), flat(dfine), dout)


def solution(mesh):
    return jax.shard_map(
        shards,
        mesh=mesh,
        in_specs=(P(None, "tile", None), P("ens", None, "tile", None)) + (P(),) * 12,
        out_specs=P("ens", None, "tile", None),
        check_vma=False,
    )
```

```python
import functools

import jax
import jax.numpy as jnp
from jax import lax
from jax.experimental import pallas as pl
from jax.experimental.pallas import tpu as pltpu
from jax.sharding import PartitionSpec as P

STEPS = 2
sigma_top = 1.0
sigma_ratio = 0.4
sigma_data = 0.5

F32 = jnp.float32
BF16 = jnp.bfloat16
HIGH = lax.Precision.HIGHEST
TILE = 8
REACH = 2


def step_gains(k):
    now = sigma_top * sigma_ratio**k
    later = sigma_top * sigma_ratio ** (k + 1) if k + 1 < STEPS else 0.0
    sq = now**2 + sigma_data**2
    return 1.0 / sq**0.5, sigma_data**2 / sq, now * sigma_data / sq**0.5, (later - now) / now


def iota2(shape, dim):
    return lax.broadcasted_iota(jnp.int32, shape, dim)


def one_hot(cond, kind=BF16):
    return jnp.where(cond, 1.0, 0.0).astype(kind)


def silu(v):
    h = 0.5 * v
    return h + h * jnp.tanh(h)


def lane_left(z):
    cols = z.shape[-1]
    half = cols // 2
    lane = iota2(z.shape, 1)
    low = jnp.where(lane == 0, 0.0, pltpu.roll(z, half + 1, 1))
    return jnp.where(lane < half, low, pltpu.roll(z, half, 1))


def lane_right(z):
    cols = z.shape[-1]
    half = cols // 2
    lane = iota2(z.shape, 1)
    high = jnp.where(lane == cols - 1, 0.0, pltpu.roll(z, half - 1, 1))
    return jnp.where(lane < half, pltpu.roll(z, half, 1), high)


def down_one(x):
    return jnp.where(iota2(x.shape, 0) == 0, 0.0, pltpu.roll(x, 1, 0))


def up_one(x):
    n = x.shape[0]
    return jnp.where(iota2(x.shape, 0) == n - 1, 0.0, pltpu.roll(x, n - 1, 0))


def store_fine(ref, row, even, odd):
    half, ch = even.shape
    e, o = even.astype(BF16), odd.astype(BF16)
    ref[row, :half, 0:ch] = down_one(odd).astype(BF16)
    ref[row, half:, 0:ch] = e
    ref[row, :half, ch : 2 * ch] = e
    ref[row, half:, ch : 2 * ch] = o
    ref[row, :half, 2 * ch :] = o
    ref[row, half:, 2 * ch :] = up_one(even).astype(BF16)


def store_coarse(ref, row, v):
    ch = v.shape[1]
    ref[row, :, 0:ch] = down_one(v).astype(BF16)
    ref[row, :, ch : 2 * ch] = v.astype(BF16)
    ref[row, :, 2 * ch :] = up_one(v).astype(BF16)


def dot(a, b):
    return jnp.dot(a, b, preferred_element_type=F32)


def kernel(n, cols, *refs):
    (cond_h, noise_h, rin_h, rdown_h, rlow_h, rup_h, rfine_h, rout_h,
     din_h, ddown_h, dlow_h, dup_h, dfine_h, dout_h, out_ref,
     cond_ref, noise_ref, rin_ref, rout_ref, din_ref, dout_ref,
     rdown, rlow, rup, rfine, ddown, dlow, dup, dfine,
     rin, rall, din, dall,
     condb, noiseb, resb, fields, top, coarse, middle, joined, zbuf, mean, res,
     wsem, csend, crecv, nsend, nrecv, rsend, rrecv) = refs
    me = lax.axis_index("tile")
    half = cols // 2
    ch = 128
    loads = [
        pltpu.make_async_copy(src, dst, wsem.at[i])
        for i, (src, dst) in enumerate(
            [(rdown_h, rdown), (rlow_h, rlow), (rup_h, rup), (rfine_h, rfine),
             (ddown_h, ddown), (dlow_h, dlow), (dup_h, dup), (dfine_h, dfine)]
        )
    ]
    small = [
        pltpu.make_async_copy(src, dst, wsem.at[8 + i])
        for i, (src, dst) in enumerate(
            [(cond_h, cond_ref), (noise_h, noise_ref), (rin_h, rin_ref), (rout_h, rout_ref),
             (din_h, din_ref), (dout_h, dout_ref)]
        )
    ]
    for copy in small:
        copy.start()
    offsets = [d for d in range(-REACH, REACH + 1) if d != 0]

    def there(d):
        return (me + d >= 0) & (me + d < n)

    barrier = pltpu.get_barrier_semaphore()
    for d in offsets:
        @pl.when(there(d))
        def _():
            pl.semaphore_signal(barrier, inc=1, device_id={"tile": me + d},
                                device_id_type=pl.DeviceIdType.MESH)
    for copy in loads:
        copy.start()

    perm = one_hot(iota2((cols, cols), 0) == 2 * (iota2((cols, cols), 1) % half) + iota2((cols, cols), 1) // half)
    perm_f = perm.astype(F32)
    nch = cond_ref.shape[0]
    shape = (TILE * 16, nch * TILE)
    m, k = iota2(shape, 0), iota2(shape, 1)
    gather = one_hot(k == (m % 16) * TILE + m // 16)
    gather = jnp.where(m % 16 < nch, gather.astype(F32), 0.0).astype(BF16)
    small[0].wait()
    own = cond_ref[...].astype(F32).reshape(nch * TILE, cols).astype(BF16)
    own = dot(gather, dot(own, perm).astype(BF16)).astype(BF16)
    condb[REACH] = own.reshape(TILE, 16, cols)
    shape = (TILE * 8, 4 * TILE)
    m, k = iota2(shape, 0), iota2(shape, 1)
    pick = jnp.where((m % 8 < 4) & (k == (m % 8) * TILE + m // 8), 1.0, 0.0)
    small[1].wait()
    noise = noise_ref[...].reshape(4 * TILE, cols)
    noise = jnp.dot(noise, perm_f, precision=HIGH, preferred_element_type=F32)
    noise = sigma_top * jnp.dot(pick, noise, precision=HIGH, preferred_element_type=F32)
    res[...] = noise
    noiseb[1] = (step_gains(0)[0] * noise).astype(BF16)
    for d in offsets:
        @pl.when(jnp.logical_not(there(d)))
        def _():
            condb[REACH + d] = jnp.zeros_like(condb[REACH + d])
            if abs(d) == 1:
                noiseb[1 + d] = jnp.zeros_like(noiseb[1 + d])
                resb[1 + d] = jnp.zeros_like(resb[1 + d])

    pl.semaphore_wait(barrier, jnp.minimum(me, REACH) + jnp.minimum(n - 1 - me, REACH))

    def cond_copy(d, incoming=False):
        return pltpu.make_async_remote_copy(
            src_ref=condb.at[REACH], dst_ref=condb.at[REACH + (d if incoming else -d)],
            send_sem=csend.at[REACH + d], recv_sem=crecv.at[REACH + (d if incoming else -d)],
            device_id={"tile": me + d}, device_id_type=pl.DeviceIdType.MESH)

    def side_copy(buf, send, recv, d, incoming=False):
        return pltpu.make_async_remote_copy(
            src_ref=buf.at[1], dst_ref=buf.at[1 + (d if incoming else -d)],
            send_sem=send.at[1 + d], recv_sem=recv.at[1 + (d if incoming else -d)],
            device_id={"tile": me + d}, device_id_type=pl.DeviceIdType.MESH)

    for d in offsets:
        @pl.when(there(d))
        def _():
            cond_copy(d).start()
    for d in (-1, 1):
        @pl.when(there(d))
        def _():
            side_copy(noiseb, nsend, nrecv, d).start()

    def place_in(src, dst, cin):
        sh = (24, cin)
        a, b = iota2(sh, 0), iota2(sh, 1)
        if cin == nch:
            take = one_hot(a == b + 8)
        else:
            want = jnp.where(b < 4, b, jnp.where(b < 4 + nch, b + 4, b - nch))
            take = one_hot(a == want)
        for y in range(3):
            parts = [dot(take, src[y, x]) for x in range(3)]
            parts.append(jnp.zeros((8, ch), F32))
            dst[y * 80 : (y + 1) * 80] = jnp.concatenate(parts, axis=0).astype(BF16)

    def place_out(src, dst, at):
        take = one_hot(iota2((8, 4), 0) == iota2((8, 4), 1) + at)
        parts = [dot(take, src[y, x]) for y in range(3) for x in range(3)]
        parts.append(jnp.zeros((8, ch), F32))
        dst[...] = jnp.concatenate(parts, axis=0).astype(BF16)

    for copy in small[2:]:
        copy.wait()
    place_in(rin_ref, rin, nch)
    place_out(rout_ref, rall, 4)
    place_in(din_ref, din, nch + 8)
    place_out(dout_ref, dall, 0)

    def put_fields(d, eight):
        wide = jnp.concatenate([eight, condb[REACH + d].astype(F32)], axis=1)
        flat = wide.reshape(TILE * 24, cols)
        left = lane_left(flat).reshape(TILE, 24, cols)
        right = lane_right(flat).reshape(TILE, 24, cols)
        both = jnp.concatenate(
            [left, wide, right, jnp.zeros((TILE, 8, cols), F32)], axis=1).astype(BF16)
        at = (REACH + d) * TILE
        fields[at : at + TILE] = both

    def unet(lo, hi, w_in, w_down, w_low, w_up, w_fine, w_all, waits):
        span = hi - lo
        first = me * TILE
        last = n * TILE

        def keep(v, g):
            return jnp.where((g + first >= 0) & (g + first < last), v, 0.0)

        def loop(count, chunk, body):
            def step(i, c):
                body(i * chunk)
                return c
            assert count % chunk == 0
            lax.fori_loop(0, count // chunk, step, 0)

        def do_top(r0):
            c = (span + 14) // 2
            parts = []
            for i in range(c):
                parts.append(jnp.concatenate(
                    [fields[r0 + (i + y + lo + 8)] for y in range(3)], axis=0))
            lhs = jnp.concatenate(parts, axis=1)
            v = silu(lax.dot_general(lhs, w_in[...], (((0,), (0,)), ((), ())),
                                     preferred_element_type=F32))
            for i in range(c):
                u = keep(v[i * cols : (i + 1) * cols], r0 + (i + lo - 7))
                store_fine(top, r0 + i, u[:half], u[half:])

        loop(span + 14, (span + 14) // 2, do_top)
        waits[0]()

        def do_coarse(r0):
            c = (span // 2 + 6) // 2
            lhs = jnp.concatenate(
                [jnp.concatenate([top[2 * r0 + 2 * i + y, :half, :] for y in range(3)], axis=1)
                 for i in range(c)], axis=0)
            v = silu(dot(lhs, w_down[...]))
            for i in range(c):
                u = keep(v[i * half : (i + 1) * half], 2 * r0 + (2 * i + lo - 6))
                store_coarse(coarse, r0 + i, u)

        loop(span // 2 + 6, (span // 2 + 6) // 2, do_coarse)
        waits[1]()

        def do_middle(r0):
            c = 8
            lhs = jnp.concatenate(
                [coarse[pl.ds(r0 + y, c)].reshape(c * half, 3 * ch) for y in range(3)], axis=1)
            v = silu(dot(lhs, w_low[...]))
            for i in range(c):
                u = keep(v[i * half : (i + 1) * half], 2 * r0 + (2 * i + lo - 4))
                store_coarse(middle, r0 + i, u)

        loop(span // 2 + 4, 8, do_middle)
        waits[2]()

        def do_joined(p0):
            c = (span // 2 + 2) // (2 if span > TILE else 1)
            rows = [middle[pl.ds(p0 + y, c)].reshape(c * half, 3 * ch) for y in range(3)]
            for ry, ((a, ka), (b, kb)) in enumerate((((0, 3), (1, 1)), ((1, 2), (2, 0)))):
                sums = []
                for at, kx in ((0, (3, 1)), (ch, (2, 0))):
                    lhs = jnp.concatenate(
                        [rows[a][:, at : at + 2 * ch], rows[b][:, at : at + 2 * ch]], axis=1)
                    rhs = jnp.concatenate(
                        [w_up[4 * ky + x] for ky in (ka, kb) for x in kx], axis=0)
                    sums.append(dot(lhs, rhs))
                for i in range(c):
                    t = 2 * p0 + (2 * i + ry)
                    g = t + (lo - 2)
                    base = top[t + 5, :, ch : 2 * ch].astype(F32)
                    even = keep(base[:half] + sums[0][i * half : (i + 1) * half], g)
                    odd = keep(base[half:] + sums[1][i * half : (i + 1) * half], g)
                    store_fine(joined, t, even, odd)

        loop(span // 2 + 2, (span // 2 + 2) // (2 if span > TILE else 1), do_joined)
        waits[3]()

        def do_refined(r0):
            c = (span + 2) // 2
            lhs = jnp.concatenate(
                [joined[pl.ds(r0 + y, c)].reshape(c * cols, 3 * ch) for y in range(3)], axis=1)
            v = silu(dot(lhs, w_fine[...]))
            for i in range(c):
                u = keep(v[i * cols : (i + 1) * cols], r0 + (i + lo - 1)).astype(BF16)
                zbuf[r0 + i] = lax.dot_general(
                    w_all[...], u, (((1,), (1,)), ((), ())), preferred_element_type=F32)

        loop(span + 2, (span + 2) // 2, do_refined)
        sums = []
        for x in range(3):
            acc = None
            for y in range(3):
                s = 8 * (3 * y + x)
                term = zbuf[y : y + span, s : s + 8, :]
                acc = term if acc is None else acc + term
            sums.append(acc.reshape(span * 8, cols))
        return lane_left(sums[0]) + sums[1] + lane_right(sums[2])

    for d in offsets:
        @pl.when(there(d))
        def _():
            cond_copy(d, True).wait_recv()
    for d in range(-REACH, REACH + 1):
        put_fields(d, jnp.zeros((TILE, 8, cols), F32))
    value = unet(-TILE, 2 * TILE, rin, rdown, rlow, rup, rfine, rall,
                 [c.wait for c in loads[:4]])
    for d in (-1, 0, 1):
        part = value[(d + 1) * 64 : (d + 2) * 64]
        mean[d + 1] = jnp.where(there(d), part, 0.0)

    nothing = lambda: None
    for step in range(STEPS):
        buf, send, recv = (noiseb, nsend, nrecv) if step == 0 else (resb, rsend, rrecv)
        in_gain, skip, gain, rate = step_gains(step)
        for d in (-1, 1):
            @pl.when(there(d))
            def _():
                side_copy(buf, send, recv, d, True).wait_recv()
        for d in (-1, 0, 1):
            put_fields(d, (buf[1 + d].astype(F32) + mean[1 + d]).reshape(TILE, 8, cols))
        net = unet(0, TILE, din, ddown, dlow, dup, dfine, dall,
                   [c.wait for c in loads[4:]] if step == 0 else [nothing] * 4)
        now = res[...]
        now = now + rate * (now - (skip * now + gain * net))
        if step + 1 < STEPS:
            res[...] = now
            resb[1] = (step_gains(step + 1)[0] * now).astype(BF16)
            for d in (-1, 1):
                @pl.when(there(d))
                def _():
                    side_copy(resb, rsend, rrecv, d).start()

    total = now + mean[1]
    shape = (4 * TILE, TILE * 8)
    m, k = iota2(shape, 0), iota2(shape, 1)
    back = jnp.where((k % 4 == m // TILE) & (k // 8 == m % TILE), 1.0, 0.0)
    total = jnp.dot(back, total, precision=HIGH, preferred_element_type=F32)
    total = lax.dot_general(total, perm_f, (((1,), (1,)), ((), ())), precision=HIGH,
                            preferred_element_type=F32)
    out_ref[...] = total.reshape(1, 4, TILE, cols)

    for d in offsets:
        @pl.when(there(d))
        def _():
            cond_copy(d).wait_send()
    for d in (-1, 1):
        @pl.when(there(d))
        def _():
            side_copy(noiseb, nsend, nrecv, d).wait_send()
            side_copy(resb, rsend, rrecv, d).wait_send()


def shards(cond, noise, rin, rdown, rlow, rup, rfine, rout, din, ddown, dlow, dup, dfine, dout):
    n = lax.axis_size("tile")
    cols = cond.shape[2]
    half = cols // 2
    ch = rdown.shape[-1]
    flat = lambda w: w.reshape(-1, ch)
    taps = lambda w: w.reshape(16, ch, ch)
    vm = pl.BlockSpec(memory_space=pltpu.VMEM)
    hb = pl.BlockSpec(memory_space=pl.ANY)
    big = (9 * ch, ch)
    wide = 3 * TILE
    dma = pltpu.SemaphoreType.DMA
    return pl.pallas_call(
        functools.partial(kernel, n, cols),
        out_shape=jax.ShapeDtypeStruct(noise.shape, F32),
        in_specs=[hb] * 14,
        out_specs=vm,
        scratch_shapes=[
            *[pltpu.VMEM(a.shape, a.dtype) for a in (cond, noise, rin, rout, din, dout)],
            *[pltpu.VMEM(s, BF16) for s in (big, big, (16, ch, ch), big) * 2],
            pltpu.VMEM((240, ch), BF16),
            pltpu.VMEM((80, ch), BF16),
            pltpu.VMEM((240, ch), BF16),
            pltpu.VMEM((80, ch), BF16),
            pltpu.VMEM((2 * REACH + 1, TILE, 16, cols), BF16),
            pltpu.VMEM((3, TILE * 8, cols), BF16),
            pltpu.VMEM((3, TILE * 8, cols), BF16),
            pltpu.VMEM((5 * TILE, 80, cols), BF16),
            pltpu.VMEM((wide + 14, cols, 3 * ch), BF16),
            pltpu.VMEM((wide // 2 + 6, half, 3 * ch), BF16),
            pltpu.VMEM((wide // 2 + 4, half, 3 * ch), BF16),
            pltpu.VMEM((wide + 4, cols, 3 * ch), BF16),
            pltpu.VMEM((wide + 2, 80, cols), F32),
            pltpu.VMEM((3, TILE * 8, cols), F32),
            pltpu.VMEM((TILE * 8, cols), F32),
            dma((14,)), dma((5,)), dma((5,)), dma((3,)), dma((3,)), dma((3,)), dma((3,)),
        ],
        compiler_params=pltpu.CompilerParams(
            collective_id=0, has_side_effects=True, vmem_limit_bytes=64 * 1024 * 1024
        ),
        cost_estimate=pl.CostEstimate(flops=4 * 10**9, bytes_accessed=3 * 10**6, transcendentals=2 * 10**6),
    )(cond, noise, rin, flat(rdown), flat(rlow), taps(rup), flat(rfine), rout,
      din, flat(ddown), flat(dlow), taps(dup), flat(dfine), dout)


def solution(mesh):
    return jax.shard_map(
        shards,
        mesh=mesh,
        in_specs=(P(None, "tile", None), P("ens", None, "tile", None)) + (P(),) * 12,
        out_specs=P("ens", None, "tile", None),
        check_vma=False,
    )
```

```python
import functools

import jax
import jax.numpy as jnp
from jax import lax
from jax.experimental import pallas as pl
from jax.experimental.pallas import tpu as pltpu
from jax.sharding import PartitionSpec as P

STEPS = 2
sigma_top = 1.0
sigma_ratio = 0.4
sigma_data = 0.5

F32 = jnp.float32
BF16 = jnp.bfloat16
HIGH = lax.Precision.HIGHEST
TILE = 8
REACH = 2
PARTS = 4


def step_gains(k):
    now = sigma_top * sigma_ratio**k
    later = sigma_top * sigma_ratio ** (k + 1) if k + 1 < STEPS else 0.0
    sq = now**2 + sigma_data**2
    return 1.0 / sq**0.5, sigma_data**2 / sq, now * sigma_data / sq**0.5, (later - now) / now


def iota2(shape, dim):
    return lax.broadcasted_iota(jnp.int32, shape, dim)


def one_hot(cond, kind=BF16):
    return jnp.where(cond, 1.0, 0.0).astype(kind)


def silu(v):
    h = 0.5 * v
    return h + h * jnp.tanh(h)


def lane_left(z):
    cols = z.shape[-1]
    half = cols // 2
    lane = iota2(z.shape, 1)
    low = jnp.where(lane == 0, 0.0, pltpu.roll(z, half + 1, 1))
    return jnp.where(lane < half, low, pltpu.roll(z, half, 1))


def lane_right(z):
    cols = z.shape[-1]
    half = cols // 2
    lane = iota2(z.shape, 1)
    high = jnp.where(lane == cols - 1, 0.0, pltpu.roll(z, half - 1, 1))
    return jnp.where(lane < half, pltpu.roll(z, half, 1), high)


def down_one(x):
    return jnp.where(iota2(x.shape, 0) == 0, 0.0, pltpu.roll(x, 1, 0))


def up_one(x):
    n = x.shape[0]
    return jnp.where(iota2(x.shape, 0) == n - 1, 0.0, pltpu.roll(x, n - 1, 0))


def store_fine(ref, row, even, odd):
    half, ch = even.shape
    e, o = even.astype(BF16), odd.astype(BF16)
    ref[row, :half, 0:ch] = down_one(odd).astype(BF16)
    ref[row, half:, 0:ch] = e
    ref[row, :half, ch : 2 * ch] = e
    ref[row, half:, ch : 2 * ch] = o
    ref[row, :half, 2 * ch :] = o
    ref[row, half:, 2 * ch :] = up_one(even).astype(BF16)


def store_coarse(ref, row, v):
    ch = v.shape[1]
    ref[row, :, 0:ch] = down_one(v).astype(BF16)
    ref[row, :, ch : 2 * ch] = v.astype(BF16)
    ref[row, :, 2 * ch :] = up_one(v).astype(BF16)


def dot(a, b):
    return jnp.dot(a, b, preferred_element_type=F32)


def kernel(n, cols, *refs):
    (cond_h, noise_h, rin_h, rdown_h, rlow_h, rup_h, rfine_h, rout_h,
     din_h, ddown_h, dlow_h, dup_h, dfine_h, dout_h, out_ref,
     cond_ref, noise_ref, rin_ref, rout_ref, din_ref, dout_ref,
     rdown, rlow, rup, rfine, ddown, dlow, dup, dfine,
     rin, rall, din, dall,
     condb, noiseb, resb, fields, top, coarse, middle, joined, zbuf, mean, res,
     meanb, wsem, csend, crecv, nsend, nrecv, rsend, rrecv, msend, mrecv) = refs
    me = lax.axis_index("tile")
    member = lax.axis_index("ens")
    part = member % PARTS
    rows_each = 3 * TILE // PARTS
    half = cols // 2
    ch = 128
    loads = [
        pltpu.make_async_copy(src, dst, wsem.at[i])
        for i, (src, dst) in enumerate(
            [(rdown_h, rdown), (rlow_h, rlow), (rup_h, rup), (rfine_h, rfine),
             (ddown_h, ddown), (dlow_h, dlow), (dup_h, dup), (dfine_h, dfine)]
        )
    ]
    small = [
        pltpu.make_async_copy(src, dst, wsem.at[8 + i])
        for i, (src, dst) in enumerate(
            [(cond_h, cond_ref), (noise_h, noise_ref), (rin_h, rin_ref), (rout_h, rout_ref),
             (din_h, din_ref), (dout_h, dout_ref)]
        )
    ]
    for copy in small:
        copy.start()
    offsets = [d for d in range(-REACH, REACH + 1) if d != 0]

    def there(d):
        return (me + d >= 0) & (me + d < n)

    barrier = pltpu.get_barrier_semaphore()
    for d in offsets:
        @pl.when(there(d))
        def _():
            pl.semaphore_signal(barrier, inc=1, device_id={"tile": me + d},
                                device_id_type=pl.DeviceIdType.MESH)
    for j in range(1, PARTS):
        pl.semaphore_signal(barrier, inc=1,
                            device_id={"ens": member - part + (part + j) % PARTS},
                            device_id_type=pl.DeviceIdType.MESH)
    for copy in loads:
        copy.start()

    perm = one_hot(iota2((cols, cols), 0) == 2 * (iota2((cols, cols), 1) % half) + iota2((cols, cols), 1) // half)
    perm_f = perm.astype(F32)
    nch = cond_ref.shape[0]
    shape = (TILE * 16, nch * TILE)
    m, k = iota2(shape, 0), iota2(shape, 1)
    gather = one_hot(k == (m % 16) * TILE + m // 16)
    gather = jnp.where(m % 16 < nch, gather.astype(F32), 0.0).astype(BF16)
    small[0].wait()
    own = cond_ref[...].astype(F32).reshape(nch * TILE, cols).astype(BF16)
    own = dot(gather, dot(own, perm).astype(BF16)).astype(BF16)
    condb[REACH] = own.reshape(TILE, 16, cols)
    shape = (TILE * 8, 4 * TILE)
    m, k = iota2(shape, 0), iota2(shape, 1)
    pick = jnp.where((m % 8 < 4) & (k == (m % 8) * TILE + m // 8), 1.0, 0.0)
    small[1].wait()
    noise = noise_ref[...].reshape(4 * TILE, cols)
    noise = jnp.dot(noise, perm_f, precision=HIGH, preferred_element_type=F32)
    noise = sigma_top * jnp.dot(pick, noise, precision=HIGH, preferred_element_type=F32)
    res[...] = noise
    noiseb[1] = (step_gains(0)[0] * noise).astype(BF16)
    for d in offsets:
        @pl.when(jnp.logical_not(there(d)))
        def _():
            condb[REACH + d] = jnp.zeros_like(condb[REACH + d])
            if abs(d) == 1:
                noiseb[1 + d] = jnp.zeros_like(noiseb[1 + d])
                resb[1 + d] = jnp.zeros_like(resb[1 + d])

    pl.semaphore_wait(barrier, jnp.minimum(me, REACH) + jnp.minimum(n - 1 - me, REACH) + (PARTS - 1))

    def cond_copy(d, incoming=False):
        return pltpu.make_async_remote_copy(
            src_ref=condb.at[REACH], dst_ref=condb.at[REACH + (d if incoming else -d)],
            send_sem=csend.at[REACH + d], recv_sem=crecv.at[REACH + (d if incoming else -d)],
            device_id={"tile": me + d}, device_id_type=pl.DeviceIdType.MESH)

    def side_copy(buf, send, recv, d, incoming=False):
        return pltpu.make_async_remote_copy(
            src_ref=buf.at[1], dst_ref=buf.at[1 + (d if incoming else -d)],
            send_sem=send.at[1 + d], recv_sem=recv.at[1 + (d if incoming else -d)],
            device_id={"tile": me + d}, device_id_type=pl.DeviceIdType.MESH)

    for d in offsets:
        @pl.when(there(d))
        def _():
            cond_copy(d).start()
    for d in (-1, 1):
        @pl.when(there(d))
        def _():
            side_copy(noiseb, nsend, nrecv, d).start()

    def place_in(src, dst, cin):
        sh = (24, cin)
        a, b = iota2(sh, 0), iota2(sh, 1)
        if cin == nch:
            take = one_hot(a == b + 8)
        else:
            want = jnp.where(b < 4, b, jnp.where(b < 4 + nch, b + 4, b - nch))
            take = one_hot(a == want)
        for y in range(3):
            parts = [dot(take, src[y, x]) for x in range(3)]
            parts.append(jnp.zeros((8, ch), F32))
            dst[y * 80 : (y + 1) * 80] = jnp.concatenate(parts, axis=0).astype(BF16)

    def place_out(src, dst, at):
        take = one_hot(iota2((8, 4), 0) == iota2((8, 4), 1) + at)
        parts = [dot(take, src[y, x]) for y in range(3) for x in range(3)]
        parts.append(jnp.zeros((8, ch), F32))
        dst[...] = jnp.concatenate(parts, axis=0).astype(BF16)

    for copy in small[2:]:
        copy.wait()
    place_in(rin_ref, rin, nch)
    place_out(rout_ref, rall, 4)
    place_in(din_ref, din, nch + 8)
    place_out(dout_ref, dall, 0)

    def put_fields(d, eight):
        wide = jnp.concatenate([eight, condb[REACH + d].astype(F32)], axis=1)
        flat = wide.reshape(TILE * 24, cols)
        left = lane_left(flat).reshape(TILE, 24, cols)
        right = lane_right(flat).reshape(TILE, 24, cols)
        both = jnp.concatenate(
            [left, wide, right, jnp.zeros((TILE, 8, cols), F32)], axis=1).astype(BF16)
        at = (REACH + d) * TILE
        fields[at : at + TILE] = both

    def unet(lo, span, w_in, w_down, w_low, w_up, w_fine, w_all, waits):
        first = me * TILE
        last = n * TILE

        def keep(v, g):
            return jnp.where((g + first >= 0) & (g + first < last), v, 0.0)

        def loop(count, chunk, body):
            def step(i, c):
                body(i * chunk)
                return c
            assert count % chunk == 0
            lax.fori_loop(0, count // chunk, step, 0)

        def do_top(r0):
            c = (span + 14) // 2
            parts = []
            for i in range(c):
                parts.append(jnp.concatenate(
                    [fields[r0 + (i + y + lo + 8)] for y in range(3)], axis=0))
            lhs = jnp.concatenate(parts, axis=1)
            v = silu(lax.dot_general(lhs, w_in[...], (((0,), (0,)), ((), ())),
                                     preferred_element_type=F32))
            for i in range(c):
                u = keep(v[i * cols : (i + 1) * cols], r0 + (i + lo - 7))
                store_fine(top, r0 + i, u[:half], u[half:])

        loop(span + 14, (span + 14) // 2, do_top)
        waits[0]()

        def do_coarse(r0):
            c = span // 2 + 6
            lhs = jnp.concatenate(
                [jnp.concatenate([top[2 * r0 + 2 * i + y, :half, :] for y in range(3)], axis=1)
                 for i in range(c)], axis=0)
            v = silu(dot(lhs, w_down[...]))
            for i in range(c):
                u = keep(v[i * half : (i + 1) * half], 2 * r0 + (2 * i + lo - 6))
                store_coarse(coarse, r0 + i, u)

        loop(span // 2 + 6, span // 2 + 6, do_coarse)
        waits[1]()

        def do_middle(r0):
            c = span // 2 + 4
            lhs = jnp.concatenate(
                [coarse[pl.ds(r0 + y, c)].reshape(c * half, 3 * ch) for y in range(3)], axis=1)
            v = silu(dot(lhs, w_low[...]))
            for i in range(c):
                u = keep(v[i * half : (i + 1) * half], 2 * r0 + (2 * i + lo - 4))
                store_coarse(middle, r0 + i, u)

        loop(span // 2 + 4, span // 2 + 4, do_middle)
        waits[2]()

        def do_joined(p0):
            c = span // 2 + 2
            rows = [middle[pl.ds(p0 + y, c)].reshape(c * half, 3 * ch) for y in range(3)]
            for ry, ((a, ka), (b, kb)) in enumerate((((0, 3), (1, 1)), ((1, 2), (2, 0)))):
                sums = []
                for at, kx in ((0, (3, 1)), (ch, (2, 0))):
                    lhs = jnp.concatenate(
                        [rows[a][:, at : at + 2 * ch], rows[b][:, at : at + 2 * ch]], axis=1)
                    rhs = jnp.concatenate(
                        [w_up[4 * ky + x] for ky in (ka, kb) for x in kx], axis=0)
                    sums.append(dot(lhs, rhs))
                for i in range(c):
                    t = 2 * p0 + (2 * i + ry)
                    g = t + (lo - 2)
                    base = top[t + 5, :, ch : 2 * ch].astype(F32)
                    even = keep(base[:half] + sums[0][i * half : (i + 1) * half], g)
                    odd = keep(base[half:] + sums[1][i * half : (i + 1) * half], g)
                    store_fine(joined, t, even, odd)

        loop(span // 2 + 2, span // 2 + 2, do_joined)
        waits[3]()

        def do_refined(r0):
            c = (span + 2) // 2
            lhs = jnp.concatenate(
                [joined[pl.ds(r0 + y, c)].reshape(c * cols, 3 * ch) for y in range(3)], axis=1)
            v = silu(dot(lhs, w_fine[...]))
            u = jnp.concatenate(
                [keep(v[i * cols : (i + 1) * cols], r0 + (i + lo - 1)).astype(BF16)
                 for i in range(c)], axis=0)
            z = lax.dot_general(
                w_all[...], u, (((1,), (1,)), ((), ())), preferred_element_type=F32)
            for i in range(c):
                zbuf[r0 + i] = z[:, i * cols : (i + 1) * cols]

        loop(span + 2, (span + 2) // 2, do_refined)
        sums = []
        for x in range(3):
            acc = None
            for y in range(3):
                s = 8 * (3 * y + x)
                term = zbuf[y : y + span, s : s + 8, :]
                acc = term if acc is None else acc + term
            sums.append(acc.reshape(span * 8, cols))
        return lane_left(sums[0]) + sums[1] + lane_right(sums[2])

    for d in offsets:
        @pl.when(there(d))
        def _():
            cond_copy(d, True).wait_recv()
    for d in range(-REACH, REACH + 1):
        put_fields(d, jnp.zeros((TILE, 8, cols), F32))
    value = unet(part * rows_each - TILE, rows_each, rin, rdown, rlow, rup, rfine, rall,
                 [c.wait for c in loads[:4]])
    meanb[part] = value

    def mean_copy(j, incoming=False):
        slot = (part + PARTS - j) % PARTS if incoming else part
        return pltpu.make_async_remote_copy(
            src_ref=meanb.at[part], dst_ref=meanb.at[slot],
            send_sem=msend.at[j], recv_sem=mrecv.at[j],
            device_id={"ens": member - part + (part + j) % PARTS},
            device_id_type=pl.DeviceIdType.MESH)

    for j in range(1, PARTS):
        mean_copy(j).start()
    for j in range(1, PARTS):
        mean_copy(j, True).wait_recv()
    value = meanb[...].reshape(3 * TILE * 8, cols)
    for d in (-1, 0, 1):
        mean[d + 1] = jnp.where(there(d), value[(d + 1) * TILE * 8 : (d + 2) * TILE * 8], 0.0)

    nothing = lambda: None
    for step in range(STEPS):
        buf, send, recv = (noiseb, nsend, nrecv) if step == 0 else (resb, rsend, rrecv)
        in_gain, skip, gain, rate = step_gains(step)
        for d in (-1, 1):
            @pl.when(there(d))
            def _():
                side_copy(buf, send, recv, d, True).wait_recv()
        for d in (-1, 0, 1):
            put_fields(d, (buf[1 + d].astype(F32) + mean[1 + d]).reshape(TILE, 8, cols))
        net = unet(0, TILE, din, ddown, dlow, dup, dfine, dall,
                   [c.wait for c in loads[4:]] if step == 0 else [nothing] * 4)
        now = res[...]
        now = now + rate * (now - (skip * now + gain * net))
        if step + 1 < STEPS:
            res[...] = now
            resb[1] = (step_gains(step + 1)[0] * now).astype(BF16)
            for d in (-1, 1):
                @pl.when(there(d))
                def _():
                    side_copy(resb, rsend, rrecv, d).start()

    total = now + mean[1]
    shape = (4 * TILE, TILE * 8)
    m, k = iota2(shape, 0), iota2(shape, 1)
    back = jnp.where((k % 4 == m // TILE) & (k // 8 == m % TILE), 1.0, 0.0)
    total = jnp.dot(back, total, precision=HIGH, preferred_element_type=F32)
    total = lax.dot_general(total, perm_f, (((1,), (1,)), ((), ())), precision=HIGH,
                            preferred_element_type=F32)
    out_ref[...] = total.reshape(1, 4, TILE, cols)

    for j in range(1, PARTS):
        mean_copy(j).wait_send()
    for d in offsets:
        @pl.when(there(d))
        def _():
            cond_copy(d).wait_send()
    for d in (-1, 1):
        @pl.when(there(d))
        def _():
            side_copy(noiseb, nsend, nrecv, d).wait_send()
            side_copy(resb, rsend, rrecv, d).wait_send()


def shards(cond, noise, rin, rdown, rlow, rup, rfine, rout, din, ddown, dlow, dup, dfine, dout):
    n = lax.axis_size("tile")
    cols = cond.shape[2]
    half = cols // 2
    ch = rdown.shape[-1]
    flat = lambda w: w.reshape(-1, ch)
    taps = lambda w: w.reshape(16, ch, ch)
    vm = pl.BlockSpec(memory_space=pltpu.VMEM)
    hb = pl.BlockSpec(memory_space=pl.ANY)
    big = (9 * ch, ch)
    assert lax.axis_size("ens") % PARTS == 0
    wide = TILE
    dma = pltpu.SemaphoreType.DMA
    return pl.pallas_call(
        functools.partial(kernel, n, cols),
        out_shape=jax.ShapeDtypeStruct(noise.shape, F32),
        in_specs=[hb] * 14,
        out_specs=vm,
        scratch_shapes=[
            *[pltpu.VMEM(a.shape, a.dtype) for a in (cond, noise, rin, rout, din, dout)],
            *[pltpu.VMEM(s, BF16) for s in (big, big, (16, ch, ch), big) * 2],
            pltpu.VMEM((240, ch), BF16),
            pltpu.VMEM((80, ch), BF16),
            pltpu.VMEM((240, ch), BF16),
            pltpu.VMEM((80, ch), BF16),
            pltpu.VMEM((2 * REACH + 1, TILE, 16, cols), BF16),
            pltpu.VMEM((3, TILE * 8, cols), BF16),
            pltpu.VMEM((3, TILE * 8, cols), BF16),
            pltpu.VMEM((5 * TILE, 80, cols), BF16),
            pltpu.VMEM((wide + 14, cols, 3 * ch), BF16),
            pltpu.VMEM((wide // 2 + 6, half, 3 * ch), BF16),
            pltpu.VMEM((wide // 2 + 4, half, 3 * ch), BF16),
            pltpu.VMEM((wide + 4, cols, 3 * ch), BF16),
            pltpu.VMEM((wide + 2, 80, cols), F32),
            pltpu.VMEM((3, TILE * 8, cols), F32),
            pltpu.VMEM((TILE * 8, cols), F32),
            pltpu.VMEM((PARTS, 3 * TILE // PARTS * 8, cols), F32),
            dma((14,)), dma((5,)), dma((5,)), dma((3,)), dma((3,)), dma((3,)), dma((3,)),
            dma((PARTS,)), dma((PARTS,)),
        ],
        compiler_params=pltpu.CompilerParams(
            collective_id=0, has_side_effects=True, vmem_limit_bytes=64 * 1024 * 1024
        ),
        cost_estimate=pl.CostEstimate(flops=4 * 10**9, bytes_accessed=3 * 10**6, transcendentals=2 * 10**6),
    )(cond, noise, rin, flat(rdown), flat(rlow), taps(rup), flat(rfine), rout,
      din, flat(ddown), flat(dlow), taps(dup), flat(dfine), dout)


def solution(mesh):
    return jax.shard_map(
        shards,
        mesh=mesh,
        in_specs=(P(None, "tile", None), P("ens", None, "tile", None)) + (P(),) * 12,
        out_specs=P("ens", None, "tile", None),
        check_vma=False,
    )
```

```python
import functools

import jax
import jax.numpy as jnp
from jax import lax
from jax.experimental import pallas as pl
from jax.experimental.pallas import tpu as pltpu
from jax.sharding import PartitionSpec as P

STEPS = 2
sigma_top = 1.0
sigma_ratio = 0.4
sigma_data = 0.5

F32 = jnp.float32
BF16 = jnp.bfloat16
HIGH = lax.Precision.HIGHEST
TILE = 8
REACH = 2


def step_gains(k):
    now = sigma_top * sigma_ratio**k
    later = sigma_top * sigma_ratio ** (k + 1) if k + 1 < STEPS else 0.0
    sq = now**2 + sigma_data**2
    return 1.0 / sq**0.5, sigma_data**2 / sq, now * sigma_data / sq**0.5, (later - now) / now


def iota2(shape, dim):
    return lax.broadcasted_iota(jnp.int32, shape, dim)


def one_hot(cond, kind=BF16):
    return jnp.where(cond, 1.0, 0.0).astype(kind)


def silu(v):
    h = 0.5 * v
    return h + h * jnp.tanh(h)


def lane_left(z):
    cols = z.shape[-1]
    half = cols // 2
    lane = iota2(z.shape, 1)
    low = jnp.where(lane == 0, 0.0, pltpu.roll(z, half + 1, 1))
    return jnp.where(lane < half, low, pltpu.roll(z, half, 1))


def lane_right(z):
    cols = z.shape[-1]
    half = cols // 2
    lane = iota2(z.shape, 1)
    high = jnp.where(lane == cols - 1, 0.0, pltpu.roll(z, half - 1, 1))
    return jnp.where(lane < half, pltpu.roll(z, half, 1), high)


def down_one(x):
    return jnp.where(iota2(x.shape, 0) == 0, 0.0, pltpu.roll(x, 1, 0))


def up_one(x):
    n = x.shape[0]
    return jnp.where(iota2(x.shape, 0) == n - 1, 0.0, pltpu.roll(x, n - 1, 0))


def store_fine(ref, row, even, odd):
    half, ch = even.shape
    e, o = even.astype(BF16), odd.astype(BF16)
    ref[row, :half, 0:ch] = down_one(odd).astype(BF16)
    ref[row, half:, 0:ch] = e
    ref[row, :half, ch : 2 * ch] = e
    ref[row, half:, ch : 2 * ch] = o
    ref[row, :half, 2 * ch :] = o
    ref[row, half:, 2 * ch :] = up_one(even).astype(BF16)


def store_coarse(ref, row, v):
    ch = v.shape[1]
    ref[row, :, 0:ch] = down_one(v).astype(BF16)
    ref[row, :, ch : 2 * ch] = v.astype(BF16)
    ref[row, :, 2 * ch :] = up_one(v).astype(BF16)


def dot(a, b):
    return jnp.dot(a, b, preferred_element_type=F32)


def kernel(n, cols, *refs):
    (cond_h, noise_h, rin_h, rdown_h, rlow_h, rup_h, rfine_h, rout_h,
     din_h, ddown_h, dlow_h, dup_h, dfine_h, dout_h, out_ref,
     cond_ref, noise_ref, rin_ref, rout_ref, din_ref, dout_ref,
     rdown, rlow, rup, rfine, ddown, dlow, dup, dfine,
     rin, rall, din, dall,
     condb, noiseb, resb, fields, top, coarse, middle, joined, zbuf, mean, res,
     wsem, csend, crecv, nsend, nrecv, rsend, rrecv) = refs
    me = lax.axis_index("tile")
    half = cols // 2
    ch = 128
    for w in (rfine, dfine):
        w[9 * ch :, :ch] = jnp.zeros((3 * ch, ch), BF16)
        w[: 3 * ch, ch:] = jnp.zeros((3 * ch, ch), BF16)
    seconds = [
        pltpu.make_async_copy(src, dst.at[3 * ch :, ch:], wsem.at[14 + i])
        for i, (src, dst) in enumerate([(rfine_h, rfine), (dfine_h, dfine)])
    ]
    loads = [
        pltpu.make_async_copy(src, dst, wsem.at[i])
        for i, (src, dst) in enumerate(
            [(rdown_h, rdown), (rlow_h, rlow), (rup_h, rup), (rfine_h, rfine.at[: 9 * ch, :ch]),
             (ddown_h, ddown), (dlow_h, dlow), (dup_h, dup), (dfine_h, dfine.at[: 9 * ch, :ch])]
        )
    ]
    small = [
        pltpu.make_async_copy(src, dst, wsem.at[8 + i])
        for i, (src, dst) in enumerate(
            [(cond_h, cond_ref), (noise_h, noise_ref), (rin_h, rin_ref), (rout_h, rout_ref),
             (din_h, din_ref), (dout_h, dout_ref)]
        )
    ]
    for copy in small:
        copy.start()
    offsets = [d for d in range(-REACH, REACH + 1) if d != 0]

    def there(d):
        return (me + d >= 0) & (me + d < n)

    barrier = pltpu.get_barrier_semaphore()
    for d in offsets:
        @pl.when(there(d))
        def _():
            pl.semaphore_signal(barrier, inc=1, device_id={"tile": me + d},
                                device_id_type=pl.DeviceIdType.MESH)
    for copy in loads + seconds:
        copy.start()

    perm = one_hot(iota2((cols, cols), 0) == 2 * (iota2((cols, cols), 1) % half) + iota2((cols, cols), 1) // half)
    perm_f = perm.astype(F32)
    nch = cond_ref.shape[0]
    shape = (TILE * 16, nch * TILE)
    m, k = iota2(shape, 0), iota2(shape, 1)
    gather = one_hot(k == (m % 16) * TILE + m // 16)
    gather = jnp.where(m % 16 < nch, gather.astype(F32), 0.0).astype(BF16)
    small[0].wait()
    own = cond_ref[...].astype(F32).reshape(nch * TILE, cols).astype(BF16)
    own = dot(gather, dot(own, perm).astype(BF16)).astype(BF16)
    condb[REACH] = own.reshape(TILE, 16, cols)
    shape = (TILE * 8, 4 * TILE)
    m, k = iota2(shape, 0), iota2(shape, 1)
    pick = jnp.where((m % 8 < 4) & (k == (m % 8) * TILE + m // 8), 1.0, 0.0)
    small[1].wait()
    noise = noise_ref[...].reshape(4 * TILE, cols)
    noise = jnp.dot(noise, perm_f, precision=HIGH, preferred_element_type=F32)
    noise = sigma_top * jnp.dot(pick, noise, precision=HIGH, preferred_element_type=F32)
    res[...] = noise
    noiseb[1] = (step_gains(0)[0] * noise).astype(BF16)
    for d in offsets:
        @pl.when(jnp.logical_not(there(d)))
        def _():
            condb[REACH + d] = jnp.zeros_like(condb[REACH + d])
            if abs(d) == 1:
                noiseb[1 + d] = jnp.zeros_like(noiseb[1 + d])
                resb[1 + d] = jnp.zeros_like(resb[1 + d])

    pl.semaphore_wait(barrier, jnp.minimum(me, REACH) + jnp.minimum(n - 1 - me, REACH))

    def cond_copy(d, incoming=False):
        return pltpu.make_async_remote_copy(
            src_ref=condb.at[REACH], dst_ref=condb.at[REACH + (d if incoming else -d)],
            send_sem=csend.at[REACH + d], recv_sem=crecv.at[REACH + (d if incoming else -d)],
            device_id={"tile": me + d}, device_id_type=pl.DeviceIdType.MESH)

    def side_copy(buf, send, recv, d, incoming=False):
        return pltpu.make_async_remote_copy(
            src_ref=buf.at[1], dst_ref=buf.at[1 + (d if incoming else -d)],
            send_sem=send.at[1 + d], recv_sem=recv.at[1 + (d if incoming else -d)],
            device_id={"tile": me + d}, device_id_type=pl.DeviceIdType.MESH)

    for d in offsets:
        @pl.when(there(d))
        def _():
            cond_copy(d).start()
    for d in (-1, 1):
        @pl.when(there(d))
        def _():
            side_copy(noiseb, nsend, nrecv, d).start()

    def place_in(src, dst, cin):
        sh = (24, cin)
        a, b = iota2(sh, 0), iota2(sh, 1)
        if cin == nch:
            take = one_hot(a == b + 8)
        else:
            want = jnp.where(b < 4, b, jnp.where(b < 4 + nch, b + 4, b - nch))
            take = one_hot(a == want)
        for y in range(3):
            parts = [dot(take, src[y, x]) for x in range(3)]
            parts.append(jnp.zeros((8, ch), F32))
            dst[y * 80 : (y + 1) * 80] = jnp.concatenate(parts, axis=0).astype(BF16)

    def place_out(src, dst, at):
        take = one_hot(iota2((8, 4), 0) == iota2((8, 4), 1) + at)
        parts = [dot(take, src[y, x]) for y in range(3) for x in range(3)]
        parts.append(jnp.zeros((8, ch), F32))
        dst[...] = jnp.concatenate(parts, axis=0).astype(BF16)

    for copy in small[2:]:
        copy.wait()
    place_in(rin_ref, rin, nch)
    place_out(rout_ref, rall, 4)
    place_in(din_ref, din, nch + 8)
    place_out(dout_ref, dall, 0)

    def put_fields(d, eight):
        wide = jnp.concatenate([eight, condb[REACH + d].astype(F32)], axis=1)
        flat = wide.reshape(TILE * 24, cols)
        left = lane_left(flat).reshape(TILE, 24, cols)
        right = lane_right(flat).reshape(TILE, 24, cols)
        both = jnp.concatenate(
            [left, wide, right, jnp.zeros((TILE, 8, cols), F32)], axis=1).astype(BF16)
        at = (REACH + d) * TILE
        fields[at : at + TILE] = both

    def unet(lo, hi, w_in, w_down, w_low, w_up, w_fine, w_all, waits):
        span = hi - lo
        first = me * TILE
        last = n * TILE

        def keep(v, g):
            return jnp.where((g + first >= 0) & (g + first < last), v, 0.0)

        def loop(count, chunk, body):
            def step(i, c):
                body(i * chunk)
                return c
            assert count % chunk == 0
            lax.fori_loop(0, count // chunk, step, 0)

        def do_top(r0):
            c = (span + 14) // 2
            parts = []
            for i in range(c):
                parts.append(jnp.concatenate(
                    [fields[r0 + (i + y + lo + 8)] for y in range(3)], axis=0))
            lhs = jnp.concatenate(parts, axis=1)
            v = silu(lax.dot_general(lhs, w_in[...], (((0,), (0,)), ((), ())),
                                     preferred_element_type=F32))
            for i in range(c):
                u = keep(v[i * cols : (i + 1) * cols], r0 + (i + lo - 7))
                store_fine(top, r0 + i, u[:half], u[half:])

        loop(span + 14, (span + 14) // 2, do_top)
        waits[0]()

        def do_coarse(r0):
            c = (span // 2 + 6) // 2
            lhs = jnp.concatenate(
                [jnp.concatenate([top[2 * r0 + 2 * i + y, :half, :] for y in range(3)], axis=1)
                 for i in range(c)], axis=0)
            v = silu(dot(lhs, w_down[...]))
            for i in range(c):
                u = keep(v[i * half : (i + 1) * half], 2 * r0 + (2 * i + lo - 6))
                store_coarse(coarse, r0 + i, u)

        loop(span // 2 + 6, (span // 2 + 6) // 2, do_coarse)
        waits[1]()

        def do_middle(r0):
            c = 8
            lhs = jnp.concatenate(
                [coarse[pl.ds(r0 + y, c)].reshape(c * half, 3 * ch) for y in range(3)], axis=1)
            v = silu(dot(lhs, w_low[...]))
            for i in range(c):
                u = keep(v[i * half : (i + 1) * half], 2 * r0 + (2 * i + lo - 4))
                store_coarse(middle, r0 + i, u)

        loop(span // 2 + 4, 8, do_middle)
        waits[2]()

        def do_joined(p0):
            c = (span // 2 + 2) // (2 if span > TILE else 1)
            rows = [middle[pl.ds(p0 + y, c)].reshape(c * half, 3 * ch) for y in range(3)]
            for ry, ((a, ka), (b, kb)) in enumerate((((0, 3), (1, 1)), ((1, 2), (2, 0)))):
                sums = []
                for at, kx in ((0, (3, 1)), (ch, (2, 0))):
                    lhs = jnp.concatenate(
                        [rows[a][:, at : at + 2 * ch], rows[b][:, at : at + 2 * ch]], axis=1)
                    rhs = jnp.concatenate(
                        [w_up[4 * ky + x] for ky in (ka, kb) for x in kx], axis=0)
                    sums.append(dot(lhs, rhs))
                for i in range(c):
                    t = 2 * p0 + (2 * i + ry)
                    g = t + (lo - 2)
                    base = top[t + 5, :, ch : 2 * ch].astype(F32)
                    even = keep(base[:half] + sums[0][i * half : (i + 1) * half], g)
                    odd = keep(base[half:] + sums[1][i * half : (i + 1) * half], g)
                    store_fine(joined, t, even, odd)

        loop(span // 2 + 2, (span // 2 + 2) // (2 if span > TILE else 1), do_joined)
        waits[3]()
        waits[4]()

        def do_refined(r0):
            c = span + 2
            lhs = jnp.concatenate(
                [jnp.concatenate([joined[r0 + (2 * i + y)] for i in range(c // 2)], axis=0)
                 for y in range(4)], axis=1)
            v = silu(dot(lhs, w_fine[...]))
            for i in range(c):
                u = v[i // 2 * cols : (i // 2 + 1) * cols, i % 2 * ch : (i % 2 + 1) * ch]
                u = keep(u, r0 + (i + lo - 1)).astype(BF16)
                zbuf[r0 + i] = lax.dot_general(
                    w_all[...], u, (((1,), (1,)), ((), ())), preferred_element_type=F32)

        loop(span + 2, span + 2, do_refined)
        sums = []
        for x in range(3):
            acc = None
            for y in range(3):
                s = 8 * (3 * y + x)
                term = zbuf[y : y + span, s : s + 8, :]
                acc = term if acc is None else acc + term
            sums.append(acc.reshape(span * 8, cols))
        return lane_left(sums[0]) + sums[1] + lane_right(sums[2])

    for d in offsets:
        @pl.when(there(d))
        def _():
            cond_copy(d, True).wait_recv()
    for d in range(-REACH, REACH + 1):
        put_fields(d, jnp.zeros((TILE, 8, cols), F32))
    value = unet(-TILE, 2 * TILE, rin, rdown, rlow, rup, rfine, rall,
                 [c.wait for c in loads[:4]] + [seconds[0].wait])
    for d in (-1, 0, 1):
        part = value[(d + 1) * 64 : (d + 2) * 64]
        mean[d + 1] = jnp.where(there(d), part, 0.0)

    nothing = lambda: None
    for step in range(STEPS):
        buf, send, recv = (noiseb, nsend, nrecv) if step == 0 else (resb, rsend, rrecv)
        in_gain, skip, gain, rate = step_gains(step)
        for d in (-1, 1):
            @pl.when(there(d))
            def _():
                side_copy(buf, send, recv, d, True).wait_recv()
        for d in (-1, 0, 1):
            put_fields(d, (buf[1 + d].astype(F32) + mean[1 + d]).reshape(TILE, 8, cols))
        net = unet(0, TILE, din, ddown, dlow, dup, dfine, dall,
                   [c.wait for c in loads[4:]] + [seconds[1].wait] if step == 0 else [nothing] * 5)
        now = res[...]
        now = now + rate * (now - (skip * now + gain * net))
        if step + 1 < STEPS:
            res[...] = now
            resb[1] = (step_gains(step + 1)[0] * now).astype(BF16)
            for d in (-1, 1):
                @pl.when(there(d))
                def _():
                    side_copy(resb, rsend, rrecv, d).start()

    total = now + mean[1]
    shape = (4 * TILE, TILE * 8)
    m, k = iota2(shape, 0), iota2(shape, 1)
    back = jnp.where((k % 4 == m // TILE) & (k // 8 == m % TILE), 1.0, 0.0)
    total = jnp.dot(back, total, precision=HIGH, preferred_element_type=F32)
    total = lax.dot_general(total, perm_f, (((1,), (1,)), ((), ())), precision=HIGH,
                            preferred_element_type=F32)
    out_ref[...] = total.reshape(1, 4, TILE, cols)

    for d in offsets:
        @pl.when(there(d))
        def _():
            cond_copy(d).wait_send()
    for d in (-1, 1):
        @pl.when(there(d))
        def _():
            side_copy(noiseb, nsend, nrecv, d).wait_send()
            side_copy(resb, rsend, rrecv, d).wait_send()


def shards(cond, noise, rin, rdown, rlow, rup, rfine, rout, din, ddown, dlow, dup, dfine, dout):
    n = lax.axis_size("tile")
    cols = cond.shape[2]
    half = cols // 2
    ch = rdown.shape[-1]
    flat = lambda w: w.reshape(-1, ch)
    taps = lambda w: w.reshape(16, ch, ch)
    vm = pl.BlockSpec(memory_space=pltpu.VMEM)
    hb = pl.BlockSpec(memory_space=pl.ANY)
    big = (9 * ch, ch)
    wide = 3 * TILE
    dma = pltpu.SemaphoreType.DMA
    return pl.pallas_call(
        functools.partial(kernel, n, cols),
        out_shape=jax.ShapeDtypeStruct(noise.shape, F32),
        in_specs=[hb] * 14,
        out_specs=vm,
        scratch_shapes=[
            *[pltpu.VMEM(a.shape, a.dtype) for a in (cond, noise, rin, rout, din, dout)],
            *[pltpu.VMEM(s, BF16) for s in (big, big, (16, ch, ch), (12 * ch, 2 * ch)) * 2],
            pltpu.VMEM((240, ch), BF16),
            pltpu.VMEM((80, ch), BF16),
            pltpu.VMEM((240, ch), BF16),
            pltpu.VMEM((80, ch), BF16),
            pltpu.VMEM((2 * REACH + 1, TILE, 16, cols), BF16),
            pltpu.VMEM((3, TILE * 8, cols), BF16),
            pltpu.VMEM((3, TILE * 8, cols), BF16),
            pltpu.VMEM((5 * TILE, 80, cols), BF16),
            pltpu.VMEM((wide + 14, cols, 3 * ch), BF16),
            pltpu.VMEM((wide // 2 + 6, half, 3 * ch), BF16),
            pltpu.VMEM((wide // 2 + 4, half, 3 * ch), BF16),
            pltpu.VMEM((wide + 4, cols, 3 * ch), BF16),
            pltpu.VMEM((wide + 2, 80, cols), F32),
            pltpu.VMEM((3, TILE * 8, cols), F32),
            pltpu.VMEM((TILE * 8, cols), F32),
            dma((16,)), dma((5,)), dma((5,)), dma((3,)), dma((3,)), dma((3,)), dma((3,)),
        ],
        compiler_params=pltpu.CompilerParams(
            collective_id=0, has_side_effects=True, vmem_limit_bytes=64 * 1024 * 1024
        ),
        cost_estimate=pl.CostEstimate(flops=4 * 10**9, bytes_accessed=3 * 10**6, transcendentals=2 * 10**6),
    )(cond, noise, rin, flat(rdown), flat(rlow), taps(rup), flat(rfine), rout,
      din, flat(ddown), flat(dlow), taps(dup), flat(dfine), dout)


def solution(mesh):
    return jax.shard_map(
        shards,
        mesh=mesh,
        in_specs=(P(None, "tile", None), P("ens", None, "tile", None)) + (P(),) * 12,
        out_specs=P("ens", None, "tile", None),
        check_vma=False,
    )
```
